32 devices in a mesh: lat: 8 (over y, x, core), lon: 4 (over z).
Axes of the slice: x: 2, y: 2, z: 4, core: 2. Of those that a mesh axis runs over, the one named last changes fastest.
Arguments:
- tokens: bfloat16 [8, 8, 128, 1024], P('lat', 'lon'), may hold values from -80 to 80
- w_qkv: bfloat16 [1024, 3072], replicated, may hold values from -0.1875 to 0.1875
- w_out: bfloat16 [1024, 1024], replicated, may hold values from -0.1875 to 0.1875
- tele_ids: int32 [8, 8, 8], P('lat', 'lon'), may hold values from 0 to 7, as said below
Outputs:
- mixed: bfloat16 [8, 8, 128, 1024], P('lat', 'lon')
The draws below stay inside these ranges and needn't reach their ends.
Inputs may be any that keep to these rules, and one draw needn't show every extreme that they name: `tele_ids`: the 16 entries of one device's query tiles name exactly 4 tile columns of each lon device, lon device o holding the tile columns o * 2 to o * 2 + 1.
All inputs are finite; a program needn't handle non-finite values.
Results may differ from the reference program's by a relative error of at most 0.013.
The reference program's roundings to bfloat16 on the way count: a program that leaves them out, or rounds other values in their place, can miss the bound.
Values may be sent and summed in bfloat16 or wider, within the bound.
No kernel may reach another device: no remote copies, remote signals or barrier semaphores. Data moves between devices by JAX's collectives and lax.ppermute only.
A program may use at most 128 MiB of HBM per device.

```python
import jax
import jax.numpy as jnp
from jax import lax

D = 1024
H = 16
HD = 64
BLOCK = 128
TELE = 8
TL = 1
TO = 2
NT_LAT = 8
NT_LON = 8
N_LAT = 8
N_LON = 4


def draw_tokens(key, part):
    full_shape = (NT_LAT, NT_LON, BLOCK, D)
    base_key = jax.random.fold_in(jax.random.fold_in(key, 3), 0)
    values = jnp.clip(jax.random.normal(base_key, full_shape, jnp.float32), -5.0, 5.0)
    return values.astype(jnp.bfloat16)


def owner_order(sub_key):
    return jax.random.permutation(sub_key, N_LON)


def draw_tele_ids(key, part):
    device_count = N_LAT * N_LON
    request_count = TL * TO * TELE
    owner_key, order_key, column_key = jax.random.split(jax.random.fold_in(key, 17), 3)
    owner_perms = jax.vmap(owner_order)(jax.random.split(owner_key, device_count))
    cycled = jnp.arange(request_count, dtype=jnp.int32) % N_LON
    owners = jnp.take(owner_perms, cycled, axis=1)

    def slot_order(sub_key):
        return jax.random.permutation(sub_key, request_count)
    orders = jax.vmap(slot_order)(jax.random.split(order_key, device_count))
    owners = jnp.take_along_axis(owners, orders, axis=1)
    columns = jax.random.randint(column_key, (device_count, request_count), 0, TO, jnp.int32)
    picks = (owners * TO + columns).astype(jnp.int32)
    picks = picks.reshape(N_LAT, N_LON, TL, TO, TELE).transpose(0, 2, 1, 3, 4)
    return picks.reshape(NT_LAT, NT_LON, TELE)


def scatter_about(rng, shape, spread, bound, kind=jnp.bfloat16):
    values = spread * jax.random.normal(rng, shape, jnp.float32)
    return jnp.clip(values, min=-bound, max=bound).astype(kind)


def setup_inputs(seed: int = 0) -> dict:
    streams_of = jax.random.split(jax.random.key(seed), 5)
    tokens = draw_tokens(jax.random.fold_in(streams_of[4], 71), 0)
    w_qkv = scatter_about(streams_of[1], (D, 3 * D), D ** -0.5, 0.1875)
    w_out = scatter_about(streams_of[2], (D, D), D ** -0.5, 0.1875)
    tele_ids = draw_tele_ids(jax.random.fold_in(streams_of[4], 71), 0)
    return {"tokens": tokens, "w_qkv": w_qkv, "w_out": w_out, "tele_ids": tele_ids}


def attend(query, pairs, usable):
    tile_count = query.shape[0]
    key_count = pairs.shape[1]
    model_width = query.shape[2]
    group_width = 2 * HD

    def one_group(group_index):
        column_start = (group_index * group_width).astype(jnp.int32)
        queries = lax.dynamic_slice_in_dim(query, column_start, group_width, 2)
        queries = queries.reshape(tile_count, BLOCK, 2, HD).astype(jnp.float32)
        key_part = lax.dynamic_slice_in_dim(pairs, column_start, group_width, 2)
        key_part = key_part.reshape(tile_count, key_count, 2, HD).astype(jnp.float32)
        value_part = lax.dynamic_slice_in_dim(pairs, model_width + column_start, group_width, 2)
        value_part = value_part.reshape(tile_count, key_count, 2, HD).astype(jnp.float32)
        scores = jnp.einsum("tqhd,tkhd->thqk", queries, key_part) * (HD ** -0.5)
        scores = jnp.where(usable[:, None, None, :], scores, -1e30)
        peak = jnp.max(scores, axis=-1, keepdims=True)
        expos = jnp.exp(scores - peak)
        weights = (expos / jnp.sum(expos, axis=-1, keepdims=True)).astype(jnp.bfloat16)
        summed = jnp.einsum("thqk,tkhd->tqhd", weights.astype(jnp.float32), value_part)
        return summed.astype(jnp.bfloat16).reshape(tile_count, BLOCK, group_width)

    outputs = lax.map(one_group, jnp.arange(H // 2, dtype=jnp.int32))
    return outputs.transpose(1, 2, 0, 3).reshape(tile_count, BLOCK, model_width)


def reference(tokens, w_qkv, w_out, tele_ids):
    model_width = tokens.shape[3]
    flat_tokens = tokens.reshape(-1, model_width)
    projected = jnp.dot(flat_tokens, w_qkv, preferred_element_type=jnp.float32).astype(jnp.bfloat16)
    projected = projected.reshape(NT_LAT, NT_LON, BLOCK, 3 * model_width)
    queries_all = projected[..., :model_width]
    pairs_all = projected[..., model_width:]
    padded = jnp.pad(pairs_all, ((1, 1), (0, 0), (0, 0), (0, 0)))

    def one_row(row_index):
        query_row = lax.dynamic_index_in_dim(queries_all, row_index, 0, keepdims=False)
        blocks = []
        flags = []
        for lat_step in range(3):
            padded_row = lax.dynamic_index_in_dim(padded, row_index + lat_step, 0, keepdims=False)
            global_row = row_index + lat_step - 1
            inside = (global_row >= 0) & (global_row < NT_LAT)
            for lon_step in (-1, 0, 1):
                blocks.append(jnp.roll(padded_row, -lon_step, axis=0))
                flags.append(jnp.full((BLOCK,), inside))
        own_row = lax.dynamic_index_in_dim(pairs_all, row_index, 0, keepdims=False)
        picks = lax.dynamic_index_in_dim(tele_ids, row_index, 0, keepdims=False)
        far_tiles = jnp.take(own_row, picks.astype(jnp.int32), axis=0)
        near_tiles = jnp.stack(blocks, axis=1)
        pairs = jnp.concatenate([near_tiles, far_tiles], axis=1)
        pairs = pairs.reshape(NT_LON, (9 + TELE) * BLOCK, 2 * model_width)
        usable = jnp.concatenate(flags + [jnp.ones((TELE * BLOCK,), jnp.bool_)])
        usable = jnp.broadcast_to(usable[None, :], (NT_LON, usable.shape[0]))
        return attend(query_row, pairs, usable)

    attended = lax.map(one_row, jnp.arange(NT_LAT, dtype=jnp.int32))
    mixed = jnp.dot(attended.reshape(-1, model_width), w_out, preferred_element_type=jnp.float32)
    return mixed.astype(jnp.bfloat16).reshape(tokens.shape)
```

```python
import functools
import jax
import jax.numpy as jnp
from jax import lax
from jax.experimental import pallas as pl
from jax.experimental.pallas import tpu as pltpu
from jax.sharding import PartitionSpec as P

HD = 64
BLOCK = 128
PAIR = 2 * HD
NEG = -1e30
CW = 256
VM = 24
UNIT = 1.4426950408889634 * HD ** -0.5


def bias_lanes(value):
    lane = lax.broadcasted_iota(jnp.int32, (BLOCK, PAIR), 1)
    whole = jnp.full((BLOCK, PAIR), value, jnp.float32)
    hi = whole.astype(jnp.bfloat16).astype(jnp.float32)
    mid = (whole - hi).astype(jnp.bfloat16).astype(jnp.float32)
    low = whole - hi - mid
    picked = jnp.where(lane == 0, hi, jnp.where(lane == 1, mid, jnp.where(lane == 2, low, 0.0)))
    return picked.astype(jnp.bfloat16)


def update(q, keys, values, bias_at, users, o_ref, m_ref, l_ref, first):
    left = lax.broadcasted_iota(jnp.int32, (BLOCK, PAIR), 1) < HD
    one = jnp.ones((2 * BLOCK, PAIR), jnp.bfloat16)
    for t in range(2):
        tiles = users[t]
        if not tiles:
            continue
        rows = slice(t * BLOCK, (t + 1) * BLOCK)
        kb = jnp.concatenate([bias_lanes(bias_at(t, j)) for j in tiles], 0)
        for pr in range(CW // PAIR):
            cols = slice(pr * PAIR, (pr + 1) * PAIR)
            qp = q[rows, cols]
            zero = jnp.zeros_like(qp)
            qbd = jnp.concatenate([jnp.where(left, qp, zero), jnp.where(left, zero, qp)], 0)
            qbd = jnp.concatenate([qbd, one], 1)
            kp = jnp.concatenate([keys[j][:, cols] for j in tiles], 0)
            kp = jnp.concatenate([kp, kb], 1)
            s = lax.dot_general(qbd, kp, (((1,), (1,)), ((), ())), preferred_element_type=jnp.float32)
            m = jnp.max(s, axis=1, keepdims=True)
            p = jnp.exp2((s - m) * UNIT).astype(jnp.bfloat16)
            vp = jnp.concatenate([values[j][:, cols] for j in tiles], 0)
            vp = jnp.concatenate([vp, jnp.ones((len(tiles) * BLOCK, PAIR), jnp.bfloat16)], 1)
            r = jnp.dot(p, vp, preferred_element_type=jnp.float32)
            o = jnp.where(left, r[:BLOCK, :PAIR], r[BLOCK:, :PAIR])
            l = jnp.where(left, r[:BLOCK, PAIR:], r[BLOCK:, PAIR:])
            m = jnp.where(left, m[:BLOCK], m[BLOCK:])
            if not first:
                m_old = m_ref[rows, cols]
                peak = jnp.maximum(m, m_old)
                was = jnp.exp2((m_old - peak) * UNIT)
                now = jnp.exp2((m - peak) * UNIT)
                o = o_ref[rows, cols] * was + o * now
                l = l_ref[rows, cols] * was + l * now
                m = peak
            o_ref[rows, cols] = o
            l_ref[rows, cols] = l
            m_ref[rows, cols] = m


def project(xs, w, off):
    flat = jnp.concatenate(xs, 0)
    return jnp.dot(flat, w[:, pl.ds(off, CW)], preferred_element_type=jnp.float32).astype(jnp.bfloat16)


def split(a):
    return [a[i:i + BLOCK] for i in range(0, a.shape[0], BLOCK)]


def groups(width, body):
    if LOOP:
        lax.fori_loop(0, width // CW, lambda i, c: (body(pl.multiple_of(i * CW, CW)), c)[1], 0)
    else:
        for i in range(width // CW):
            body(i * CW)


LOOP = False


def first_kernel(base, bias_ref, x_ref, w, q_ref, o_ref, m_ref, l_ref):
    width = x_ref.shape[-1]

    def body(off):
        here = pl.ds(off, CW)
        xs = [x_ref[j] for j in range(2)]
        q = project(xs, w, off)
        q_ref[:, here] = q
        keys, values = split(project(xs, w, width + off)), split(project(xs, w, 2 * width + off))
        update(q, keys, values, lambda t, j: bias_ref[t, base + j], [[0, 1], [0, 1]],
               o_ref.at[:, here], m_ref.at[:, here], l_ref.at[:, here], True)

    groups(width, body)


def step_kernel(base, users, counts, bias_ref, *refs):
    x_refs, (q_ref, w, o_in, m_in, l_in, o_ref, m_ref, l_ref) = refs[:len(counts)], refs[len(counts):]
    width = q_ref.shape[-1]

    def body(off):
        here = pl.ds(off, CW)
        xs = [r[j] for r, n in zip(x_refs, counts) for j in range(n)]
        keys, values = split(project(xs, w, width + off)), split(project(xs, w, 2 * width + off))
        update(q_ref[:, here], keys, values, lambda t, j: bias_ref[t, base + j], users,
               o_ref.at[:, here], m_ref.at[:, here], l_ref.at[:, here], False)

    groups(width, body)


def last_kernel(base, users, counts, bias_ref, *refs):
    x_refs, (q_ref, w, w_out, o_in, m_in, l_in, out_ref, o_ref, m_ref, l_ref, acc) = refs[:len(counts)], refs[len(counts):]
    width = q_ref.shape[-1]
    acc[...] = jnp.zeros_like(acc)

    def body(off):
        here = pl.ds(off, CW)
        xs = [r[j] for r, n in zip(x_refs, counts) for j in range(n)]
        keys, values = split(project(xs, w, width + off)), split(project(xs, w, 2 * width + off))
        update(q_ref[:, here], keys, values, lambda t, j: bias_ref[t, base + j], users,
               o_ref.at[:, here], m_ref.at[:, here], l_ref.at[:, here], False)
        att = (o_ref[:, here] / l_ref[:, here]).astype(jnp.bfloat16)
        acc[...] += jnp.dot(att, w_out[here, :], preferred_element_type=jnp.float32)

    groups(width, body)
    out_ref[...] = acc[...].astype(jnp.bfloat16)


PARAMS = pltpu.CompilerParams(vmem_limit_bytes=VM * 1024 * 1024)
SMEM = pl.BlockSpec(memory_space=pltpu.SMEM)
VMEM = pl.BlockSpec(memory_space=pltpu.VMEM)


def state_shapes(width):
    return [jax.ShapeDtypeStruct((2 * BLOCK, width), jnp.float32)] * 3


def run_first(base, bias, x, w_qkv):
    width = x.shape[-1]
    return pl.pallas_call(
        functools.partial(first_kernel, base),
        in_specs=[SMEM] + [VMEM] * 2, out_specs=[VMEM] * 4,
        out_shape=[jax.ShapeDtypeStruct((2 * BLOCK, width), jnp.bfloat16)] + state_shapes(width),
        compiler_params=PARAMS, name="own",
    )(bias, x, w_qkv)


def run_step(base, users, bias, xs, q, w_qkv, state, name):
    width = q.shape[-1]
    counts = [x.shape[0] for x in xs]
    n = len(xs)
    return pl.pallas_call(
        functools.partial(step_kernel, base, users, counts),
        in_specs=[SMEM] + [VMEM] * (n + 5), out_specs=[VMEM] * 3, out_shape=state_shapes(width),
        input_output_aliases={n + 3: 0, n + 4: 1, n + 5: 2},
        compiler_params=PARAMS, name=name,
    )(bias, *xs, q, w_qkv, *state)


def run_last(base, users, bias, xs, q, w_qkv, w_out, state):
    width = q.shape[-1]
    counts = [x.shape[0] for x in xs]
    n = len(xs)
    return pl.pallas_call(
        functools.partial(last_kernel, base, users, counts),
        in_specs=[SMEM] + [VMEM] * (n + 6), out_specs=[VMEM] * 4,
        out_shape=[jax.ShapeDtypeStruct((2 * BLOCK, width), jnp.bfloat16)] + state_shapes(width),
        input_output_aliases={n + 4: 1, n + 5: 2, n + 6: 3},
        scratch_shapes=[pltpu.VMEM((2 * BLOCK, width), jnp.float32)],
        compiler_params=PARAMS, name="last",
    )(bias, *xs, q, w_qkv, w_out, *state)[0]


BOTH = [[0, 1], [0, 1]]


def pass_on(array, axis, pairs):
    return lax.ppermute(array, axis, pairs)


def make_bias(tele_ids, columns, usable, in_row, own_first, total):
    query_column = (own_first + jnp.arange(2, dtype=jnp.int32))[:, None]
    told = (tele_ids[:, None, :] == columns[None, :, None]).sum(-1)
    beside = lax.rem(columns[None, :] - query_column + 1 + total, total) <= 2
    times = jnp.where(in_row[None, :], told + beside, 1) * usable[None, :]
    logs = jnp.log(jnp.maximum(times, 1).astype(jnp.float32)) * HD ** 0.5
    return jnp.where(times > 0, logs, NEG)


def lat_swap(array, n_lat):
    same = [(i, i ^ 1) for i in range(n_lat)]
    other = [p for i in range(1, n_lat - 1, 2) for p in ((i, i + 1), (i + 1, i))]
    return pass_on(array, "lat", same), pass_on(array, "lat", other)


def on_device(tokens, w_qkv, w_out, tele_ids):
    n_lat, n_lon = lax.axis_size("lat"), lax.axis_size("lon")
    total = 2 * n_lon
    a, z = lax.axis_index("lat"), lax.axis_index("lon")
    x = tokens[0]
    first, last = z == 0, z == n_lon - 1
    edge_ok = jnp.where(a % 2 == 0, a > 0, a < n_lat - 1)
    i32 = lambda *v: jnp.stack([jnp.asarray(u, jnp.int32) for u in v])
    b = 2 * z
    yes = jnp.int32(1)
    if n_lon == 4:
        across = lax.rem(z + 2, 4) * 2
        columns = i32(b, b + 1, 0, 0, 0, 0, b - 2, b - 1, b + 2, b + 3,
                      jnp.where(first, total - 1, 0), 0, 0, 0, 0, across, across + 1, jnp.where(first, total - 2, 1))
        ends = first | last
        usable = i32(yes, yes, yes, yes, edge_ok, edge_ok, ~first, ~first, ~last, ~last,
                     ends, yes, yes, edge_ok, edge_ok, yes, yes, ends)
        in_row = jnp.array([1, 1, 0, 0, 0, 0, 1, 1, 1, 1, 1, 0, 0, 0, 0, 1, 1, 1], jnp.bool_)
    else:
        everywhere = jnp.arange(total, dtype=jnp.int32)
        columns = jnp.concatenate([i32(b, b + 1, 0, 0, 0, 0, 0, 0, 0, 0), everywhere])
        not_own = ((everywhere < b) | (everywhere > b + 1)).astype(jnp.int32)
        usable = jnp.concatenate([i32(yes, yes, yes, yes, edge_ok, edge_ok, yes, yes, edge_ok, edge_ok), not_own])
        in_row = jnp.array([1, 1] + [0] * 8 + [1] * total, jnp.bool_)
    bias = make_bias(tele_ids[0], columns, usable, in_row, b, total)

    if n_lon == 4:
        wrap = pass_on(jnp.where(first, x[0], x[1])[None], "lon", [(0, 3), (3, 0)])
        up1 = pass_on(x, "lon", [(i, i + 1) for i in range(3)])
        down1 = pass_on(x, "lon", [(i + 1, i) for i in range(3)])
    same, other = lat_swap(x, n_lat)
    q, *state = run_first(0, bias, x, w_qkv)
    state = run_step(2, [[0, 1, 2, 3]] * 2, bias, [same, other], q, w_qkv, state, "rim_own")
    if n_lon == 4:
        up2 = pass_on(up1, "lon", [(1, 2), (2, 3)])
        down2 = pass_on(down1, "lon", [(2, 1), (1, 0)])
        edges = jnp.concatenate([jnp.where(first, wrap, up1[1:]), jnp.where(last, wrap, down1[:1])], 0)
        same_edges, other_edges = lat_swap(edges, n_lat)
        state = run_step(6, [[0, 1, 2, 3]] * 2, bias, [up1, down1], q, w_qkv, state, "beside")
        state = run_step(10, [[0, 1, 3], [0, 2, 4]], bias, [wrap, same_edges, other_edges], q, w_qkv, state, "rim_edge")
        far = jnp.where(z < 2, down2, up2)
        final = pass_on(jnp.where(z < 2, down2[:1], up2[1:]), "lon", [(1, 0), (2, 3)])
        state = run_step(15, BOTH, bias, [far], q, w_qkv, state, "across")
        mixed = run_last(17, [[0], [0]], bias, [final], q, w_qkv, w_out, state)
    else:
        before = pass_on(x[1:], "lon", [(i, (i + 1) % n_lon) for i in range(n_lon)])
        after = pass_on(x[:1], "lon", [((i + 1) % n_lon, i) for i in range(n_lon)])
        same_edges, other_edges = lat_swap(jnp.concatenate([before, after], 0), n_lat)
        state = run_step(6, [[0, 2], [1, 3]], bias, [same_edges, other_edges], q, w_qkv, state, "rim_edge")
        row = lax.all_gather(x, "lon", axis=0, tiled=True)
        for s in range(0, total, 4):
            args = (10 + s, [[0, 1, 2, 3]] * 2, bias, [row[s:s + 4]], q, w_qkv)
            if s + 4 < total:
                state = run_step(*args, state, "columns")
        mixed = run_last(*args, w_out, state)
    return mixed.reshape(tokens.shape)


def solution(mesh):
    return jax.shard_map(
        on_device,
        mesh=mesh,
        in_specs=(P("lat", "lon", None, None), P(), P(), P("lat", "lon", None)),
        out_specs=P("lat", "lon", None, None),
        check_vma=False,
    )
```

```python
import functools
import math
import jax
import jax.numpy as jnp
from jax import lax
from jax.experimental import pallas as pl
from jax.experimental.pallas import tpu as pltpu
from jax.sharding import PartitionSpec as P

HD = 64
BLOCK = 128
PAIR = 2 * HD
NEG = -1e30
CW = 256
VM = 24
COST = 1_200_000_000
UNIT = 1.4426950408889634 * HD ** -0.5


def log_times(times):
    value = jnp.float32(NEG)
    for k in range(1, 12):
        value = jnp.where(times == k, jnp.float32(math.log(k) * HD ** 0.5), value)
    return value


def row_bias(tele_ref, own, total, column, t):
    told = jnp.int32(0)
    for k in range(tele_ref.shape[2]):
        told = told + (tele_ref[0, t, k] == column).astype(jnp.int32)
    beside = lax.rem(column - (own + t) + 1 + total, total) <= 2
    return log_times(told + beside.astype(jnp.int32))


def bias_lanes(value):
    lane = lax.broadcasted_iota(jnp.int32, (BLOCK, PAIR), 1)
    whole = jnp.full((BLOCK, PAIR), value, jnp.float32)
    hi = whole.astype(jnp.bfloat16).astype(jnp.float32)
    mid = (whole - hi).astype(jnp.bfloat16).astype(jnp.float32)
    low = whole - hi - mid
    picked = jnp.where(lane == 0, hi, jnp.where(lane == 1, mid, jnp.where(lane == 2, low, 0.0)))
    return picked.astype(jnp.bfloat16)


def update(q, keys, values, bias, users, o_ref, m_ref, l_ref, first):
    left = lax.broadcasted_iota(jnp.int32, (BLOCK, PAIR), 1) < HD
    one = jnp.ones((2 * BLOCK, PAIR), jnp.bfloat16)
    for t in range(2):
        tiles = users[t]
        if not tiles:
            continue
        rows = slice(t * BLOCK, (t + 1) * BLOCK)
        kb = jnp.concatenate([bias_lanes(bias[t][j]) for j in tiles], 0)
        for pr in range(CW // PAIR):
            cols = slice(pr * PAIR, (pr + 1) * PAIR)
            qp = q[rows, cols]
            zero = jnp.zeros_like(qp)
            qbd = jnp.concatenate([jnp.where(left, qp, zero), jnp.where(left, zero, qp)], 0)
            qbd = jnp.concatenate([qbd, one], 1)
            kp = jnp.concatenate([keys[j][:, cols] for j in tiles], 0)
            kp = jnp.concatenate([kp, kb], 1)
            s = lax.dot_general(qbd, kp, (((1,), (1,)), ((), ())), preferred_element_type=jnp.float32)
            m = jnp.max(s, axis=1, keepdims=True)
            p = jnp.exp2((s - m) * UNIT).astype(jnp.bfloat16)
            vp = jnp.concatenate([values[j][:, cols] for j in tiles], 0)
            vp = jnp.concatenate([vp, jnp.ones((len(tiles) * BLOCK, PAIR), jnp.bfloat16)], 1)
            r = jnp.dot(p, vp, preferred_element_type=jnp.float32)
            o = jnp.where(left, r[:BLOCK, :PAIR], r[BLOCK:, :PAIR])
            l = jnp.where(left, r[:BLOCK, PAIR:], r[BLOCK:, PAIR:])
            m = jnp.where(left, m[:BLOCK], m[BLOCK:])
            if not first:
                m_old = m_ref[rows, cols]
                peak = jnp.maximum(m, m_old)
                was = jnp.exp2((m_old - peak) * UNIT)
                now = jnp.exp2((m - peak) * UNIT)
                o = o_ref[rows, cols] * was + o * now
                l = l_ref[rows, cols] * was + l * now
                m = peak
            o_ref[rows, cols] = o
            l_ref[rows, cols] = l
            m_ref[rows, cols] = m


def project(xs, w, off):
    flat = jnp.concatenate(xs, 0)
    return jnp.dot(flat, w[:, pl.ds(off, CW)], preferred_element_type=jnp.float32).astype(jnp.bfloat16)


def split(a):
    return [a[i:i + BLOCK] for i in range(0, a.shape[0], BLOCK)]


def groups(width, body):
    if LOOP:
        lax.fori_loop(0, width // CW, lambda i, c: (body(pl.multiple_of(i * CW, CW)), c)[1], 0)
    else:
        for i in range(width // CW):
            body(i * CW)


LOOP = False


class Place:
    def __init__(self, tele_ref, n_lat, n_lon):
        self.tele_ref, self.n_lon = tele_ref, n_lon
        a, self.z = lax.axis_index("lat"), lax.axis_index("lon")
        self.first, self.last = self.z == 0, self.z == n_lon - 1
        self.other_ok = jnp.where(lax.rem(a, 2) == 0, a > 0, a < n_lat - 1)

    def row(self, column):
        return [row_bias(self.tele_ref, 2 * self.z, 2 * self.n_lon, column, t) for t in range(2)]

    def rim(self, same):
        value = jnp.float32(0.0) if same else jnp.where(self.other_ok, jnp.float32(0.0), jnp.float32(NEG))
        return [value, value]


def attend_kernel(gather, users, n_x, kind, place, tele_ref, *refs):
    x_refs, refs = refs[:n_x], refs[n_x:]
    at = Place(tele_ref, *place)
    xs, tiles_bias = gather(at, *x_refs)
    bias = [[both[t] for both in tiles_bias] for t in range(2)]
    width = xs[0].shape[-1]
    if kind == "first":
        w, q_ref, o_ref, m_ref, l_ref = refs
    elif kind == "last":
        q_ref, w, w_out, o_in, m_in, l_in, out_ref, o_ref, m_ref, l_ref, att = refs
    else:
        q_ref, w, o_in, m_in, l_in, o_ref, m_ref, l_ref = refs

    def body(off):
        here = pl.ds(off, CW)
        if kind == "first":
            q = project(xs[:2], w, off)
            q_ref[:, here] = q
        else:
            q = q_ref[:, here]
        keys, values = split(project(xs, w, width + off)), split(project(xs, w, 2 * width + off))
        update(q, keys, values, bias, users, o_ref.at[:, here], m_ref.at[:, here], l_ref.at[:, here], kind == "first")
        if kind == "last":
            att[:, here] = (o_ref[:, here] / l_ref[:, here]).astype(jnp.bfloat16)

    groups(width, body)
    if kind == "last":
        out_ref[...] = jnp.dot(att[...], w_out[...], preferred_element_type=jnp.float32).astype(jnp.bfloat16)


SMEM = pl.BlockSpec(memory_space=pltpu.SMEM)
VMEM = pl.BlockSpec(memory_space=pltpu.VMEM)


def state_shapes(width):
    return [jax.ShapeDtypeStruct((2 * BLOCK, width), jnp.float32)] * 3


def attend(gather, users, tiles, place, tele_ids, xs, w_qkv, name, q=None, state=None, w_out=None):
    kind = "first" if state is None else "step" if w_out is None else "last"
    width = xs[0].shape[-1]
    q_shape = jax.ShapeDtypeStruct((2 * BLOCK, width), jnp.bfloat16)
    out_shape = state_shapes(width)
    args = [tele_ids, *xs]
    aliases, scratch = {}, []
    if kind == "first":
        args += [w_qkv]
        out_shape = [q_shape] + out_shape
    else:
        args += [q, w_qkv] + ([w_out] if kind == "last" else []) + list(state)
        out_shape = ([q_shape] if kind == "last" else []) + out_shape
        aliases = {len(args) - 3 + k: len(out_shape) - 3 + k for k in range(3)}
        if kind == "last":
            scratch = [pltpu.VMEM((2 * BLOCK, width), jnp.bfloat16)]
    spent = tiles * COST
    return pl.pallas_call(
        functools.partial(attend_kernel, gather, users, len(xs), kind, place),
        in_specs=[SMEM] + [VMEM] * (len(args) - 1), out_specs=[VMEM] * len(out_shape), out_shape=out_shape,
        input_output_aliases=aliases, scratch_shapes=scratch, name=name,
        compiler_params=pltpu.CompilerParams(vmem_limit_bytes=VM * 1024 * 1024),
        cost_estimate=pl.CostEstimate(flops=spent, bytes_accessed=tiles * 500_000, transcendentals=0),
    )(*args)


def gate_kernel(count, *refs):
    del count, refs


def gate(arrays, after):
    count = len(arrays)
    return pl.pallas_call(
        functools.partial(gate_kernel, count),
        in_specs=[pl.BlockSpec(memory_space=pl.ANY)] * (count + len(after)),
        out_specs=[pl.BlockSpec(memory_space=pl.ANY)] * count,
        out_shape=[jax.ShapeDtypeStruct(v.shape, v.dtype) for v in arrays],
        input_output_aliases={k: k for k in range(count)}, name="gate",
        compiler_params=pltpu.CompilerParams(vmem_limit_bytes=1024 * 1024),
    )(*arrays, *after)


PAIRS = [[0, 1], [0, 1]]
BOTH = [[0, 1, 2, 3], [0, 1, 2, 3]]


def lat_swap(array, n_lat):
    same = [(i, i ^ 1) for i in range(n_lat)]
    other = [p for i in range(1, n_lat - 1, 2) for p in ((i, i + 1), (i + 1, i))]
    return lax.ppermute(array, "lat", same), lax.ppermute(array, "lat", other)


def own_alone(at, x):
    b = 2 * at.z
    return [x[0], x[1]], [at.row(b), at.row(b + 1)]


def lon_step(at, which):
    step = jnp.where(lax.rem(at.z, 2) == which, 1, -1)
    b = 2 * lax.rem(at.z + step + at.n_lon, at.n_lon)
    return [at.row(b), at.row(b + 1)]


def near_tiles(at, near, ring, same, other):
    return ([near[0], near[1], ring[0], ring[1], same[0], same[1], other[0], other[1]],
            lon_step(at, 0) + lon_step(at, 1) + [at.rim(True)] * 2 + [at.rim(False)] * 2)


def corner_tiles(at, same, other):
    return [same[0], other[0], same[1], other[1]], [at.rim(True), at.rim(False)] * 2


def across_tiles(at, far):
    b = lax.rem(2 * at.z + 4, 8)
    return [far[0], far[1]], [at.row(b), at.row(b + 1)]


def rim_tiles(at, same, other, same_edges, other_edges):
    return ([same[0], same[1], other[0], other[1], same_edges[0], same_edges[1], other_edges[0], other_edges[1]],
            [at.rim(True)] * 2 + [at.rim(False)] * 2 + [at.rim(True)] * 2 + [at.rim(False)] * 2)


def column_tiles(start, at, row):
    found = []
    for j in range(row.shape[0]):
        own = (start + j >= 2 * at.z) & (start + j <= 2 * at.z + 1)
        found.append([jnp.where(own, jnp.float32(NEG), v) for v in at.row(jnp.int32(start + j))])
    return [row[j] for j in range(row.shape[0])], found


def on_device(tokens, w_qkv, w_out, tele_ids):
    n_lat, n_lon = lax.axis_size("lat"), lax.axis_size("lon")
    place = (n_lat, n_lon)
    z = lax.axis_index("lon")
    x = tokens[0]
    if n_lon == 4:
        near_pairs = [(i, i ^ 1) for i in range(4)]
        same, other = lat_swap(x, n_lat)
        ring = lax.ppermute(x, "lon", [(0, 3), (3, 0), (1, 2), (2, 1)])
        near = lax.ppermute(x, "lon", near_pairs)
        q, *state = attend(own_alone, PAIRS, 3, place, tele_ids, [x], w_qkv, "own")
        near, ring, same, other = gate([near, ring, same, other], [state[0]])
        even = lax.rem(z, 2) == 0
        edges = jnp.concatenate([jnp.where(even, ring[1:], near[1:]), jnp.where(even, near[:1], ring[:1])], 0)
        same_edges, other_edges = lat_swap(edges, n_lat)
        far = lax.ppermute(ring, "lon", near_pairs)
        state = attend(near_tiles, [list(range(8))] * 2, 8, place, tele_ids, [near, ring, same, other], w_qkv, "near", q, state)
        state = attend(corner_tiles, [[0, 1], [2, 3]], 4, place, tele_ids,
                       [same_edges, other_edges], w_qkv, "corner", q, state)
        mixed = attend(across_tiles, PAIRS, 3, place, tele_ids, [far], w_qkv, "across", q, state, w_out)[0]
    else:
        q, *state = attend(own_alone, PAIRS, 2, place, tele_ids, [x], w_qkv, "own")
        same, other = lat_swap(x, n_lat)
        before = lax.ppermute(x[1:], "lon", [(i, (i + 1) % n_lon) for i in range(n_lon)])
        after = lax.ppermute(x[:1], "lon", [((i + 1) % n_lon, i) for i in range(n_lon)])
        same_edges, other_edges = lat_swap(jnp.concatenate([before, after], 0), n_lat)
        state = attend(rim_tiles, [[0, 1, 2, 3, 4, 6], [0, 1, 2, 3, 5, 7]], 8, place, tele_ids,
                       [same, other, same_edges, other_edges], w_qkv, "rim", q, state)
        row = lax.all_gather(x, "lon", axis=0, tiled=True)
        for s in range(0, 2 * n_lon, 4):
            state = attend(functools.partial(column_tiles, s), BOTH, 4, place, tele_ids, [row[s:s + 4]], w_qkv,
                           "columns", q, state, w_out if s + 4 == 2 * n_lon else None)
        mixed = state[0]
    return mixed.reshape(tokens.shape)


def solution(mesh):
    return jax.shard_map(
        on_device,
        mesh=mesh,
        in_specs=(P("lat", "lon", None, None), P(), P(), P("lat", "lon", None)),
        out_specs=P("lat", "lon", None, None),
        check_vma=False,
    )
```

```python
import functools
import math
import jax
import jax.numpy as jnp
from jax import lax
from jax.experimental import pallas as pl
from jax.experimental.pallas import tpu as pltpu
from jax.sharding import PartitionSpec as P

HD = 64
BLOCK = 128
PAIR = 2 * HD
NEG = -1e30
CW = 256
VM = 24
COST = 0
UNIT = 1.4426950408889634 * HD ** -0.5


def log_times(times):
    value = jnp.float32(NEG)
    for k in range(1, 12):
        value = jnp.where(times == k, jnp.float32(math.log(k) * HD ** 0.5), value)
    return value


def row_bias(tele_ref, own, total, column, t):
    told = jnp.int32(0)
    for k in range(tele_ref.shape[2]):
        told = told + (tele_ref[0, t, k] == column).astype(jnp.int32)
    beside = lax.rem(column - (own + t) + 1 + total, total) <= 2
    return log_times(told + beside.astype(jnp.int32))


def bias_lanes(values):
    lane = lax.broadcasted_iota(jnp.int32, (BLOCK, PAIR), 1)
    picked = jnp.zeros((BLOCK, PAIR), jnp.float32)
    for t, value in enumerate(values):
        whole = jnp.full((BLOCK, PAIR), value, jnp.float32)
        hi = whole.astype(jnp.bfloat16).astype(jnp.float32)
        mid = (whole - hi).astype(jnp.bfloat16).astype(jnp.float32)
        for k, part in enumerate((hi, mid, whole - hi - mid)):
            picked = jnp.where(lane == 3 * t + k, part, picked)
    return picked.astype(jnp.bfloat16)


def stacked(parts):
    return parts[0] if len(parts) == 1 else jnp.concatenate(parts, 0)


def update(q, keys, values, bias, users, o_ref, m_ref, l_ref, first):
    if users[0] == users[1]:
        update_some(q, keys, values, bias, users, o_ref, m_ref, l_ref, first, (0, 1))
    else:
        for t in range(2):
            update_some(q, keys, values, bias, users, o_ref, m_ref, l_ref, first, (t,))


def update_some(q, keys, values, bias, users, o_ref, m_ref, l_ref, first, which):
    lane = lax.broadcasted_iota(jnp.int32, (BLOCK, PAIR), 1)
    left = lane < HD
    picks = [((lane >= 3 * t) & (lane < 3 * t + 3)).astype(jnp.float32).astype(jnp.bfloat16) for t in range(2)]
    tiles = users[which[0]]
    lanes = [bias_lanes([bias[t][j] for t in range(2)]) for j in tiles]
    rows = [slice(t * BLOCK, (t + 1) * BLOCK) for t in range(2)]
    two = 2 * BLOCK
    for pr in range(CW // PAIR):
        cols = slice(pr * PAIR, (pr + 1) * PAIR)
        wide = []
        for t in which:
            qp = q[rows[t], cols]
            zero = jnp.zeros_like(qp)
            both = jnp.concatenate([jnp.where(left, qp, zero), jnp.where(left, zero, qp)], 0)
            wide.append(jnp.concatenate([both, jnp.concatenate([picks[t], picks[t]], 0)], 1))
        kp = stacked([jnp.concatenate([keys[j][:, cols], b], 1) for j, b in zip(tiles, lanes)])
        s = lax.dot_general(stacked(wide), kp, (((1,), (1,)), ((), ())), preferred_element_type=jnp.float32)
        peaks = jnp.max(s, axis=1, keepdims=True)
        p = jnp.exp2((s - peaks) * UNIT).astype(jnp.bfloat16)
        vp = stacked([values[j][:, cols] for j in tiles])
        vp = jnp.concatenate([vp, jnp.ones((len(tiles) * BLOCK, PAIR), jnp.bfloat16)], 1)
        sums = jnp.dot(p, vp, preferred_element_type=jnp.float32)
        for i, t in enumerate(which):
            r, m = sums[i * two:(i + 1) * two], peaks[i * two:(i + 1) * two]
            o = jnp.where(left, r[:BLOCK, :PAIR], r[BLOCK:, :PAIR])
            l = jnp.where(left, r[:BLOCK, PAIR:], r[BLOCK:, PAIR:])
            m = jnp.where(left, m[:BLOCK], m[BLOCK:])
            if not first:
                m_old = m_ref[rows[t], cols]
                peak = jnp.maximum(m, m_old)
                was = jnp.exp2((m_old - peak) * UNIT)
                now = jnp.exp2((m - peak) * UNIT)
                o = o_ref[rows[t], cols] * was + o * now
                l = l_ref[rows[t], cols] * was + l * now
                m = peak
            o_ref[rows[t], cols] = o
            l_ref[rows[t], cols] = l
            m_ref[rows[t], cols] = m


def project(xs, w, off):
    flat = jnp.concatenate(xs, 0)
    return jnp.dot(flat, w[:, pl.ds(off, CW)], preferred_element_type=jnp.float32).astype(jnp.bfloat16)


def split(a):
    return [a[i:i + BLOCK] for i in range(0, a.shape[0], BLOCK)]


def groups(width, body):
    if LOOP:
        lax.fori_loop(0, width // CW, lambda i, c: (body(pl.multiple_of(i * CW, CW)), c)[1], 0)
    else:
        for i in range(width // CW):
            body(i * CW)


LOOP = False


class Place:
    def __init__(self, tele_ref, n_lat, n_lon):
        self.tele_ref, self.n_lon = tele_ref, n_lon
        a, self.z = lax.axis_index("lat"), lax.axis_index("lon")
        self.first, self.last = self.z == 0, self.z == n_lon - 1
        self.other_ok = jnp.where(lax.rem(a, 2) == 0, a > 0, a < n_lat - 1)

    def row(self, column):
        return [row_bias(self.tele_ref, 2 * self.z, 2 * self.n_lon, column, t) for t in range(2)]

    def rim(self, same):
        value = jnp.float32(0.0) if same else jnp.where(self.other_ok, jnp.float32(0.0), jnp.float32(NEG))
        return [value, value]


def attend_kernel(gather, users, n_x, kind, place, tele_ref, *refs):
    x_refs, refs = refs[:n_x], refs[n_x:]
    at = Place(tele_ref, *place)
    xs, tiles_bias = gather(at, *x_refs)
    bias = [[both[t] for both in tiles_bias] for t in range(2)]
    width = xs[0].shape[-1]
    if kind == "first":
        w, q_ref, rest_ref, o_ref, m_ref, l_ref = refs
        rest_ref[0] = jnp.where(lax.rem(at.z, 2) == 0, x_refs[0][1], x_refs[0][0])
    elif kind == "last":
        q_ref, w, w_out, o_in, m_in, l_in, out_ref, o_ref, m_ref, l_ref, att = refs
    else:
        q_ref, w, o_in, m_in, l_in, o_ref, m_ref, l_ref = refs

    def body(off):
        here = pl.ds(off, CW)
        if kind == "first":
            q = project(xs[:2], w, off)
            q_ref[:, here] = q
        else:
            q = q_ref[:, here]
        keys, values = split(project(xs, w, width + off)), split(project(xs, w, 2 * width + off))
        update(q, keys, values, bias, users, o_ref.at[:, here], m_ref.at[:, here], l_ref.at[:, here], kind == "first")
        if kind == "last":
            att[:, here] = (o_ref[:, here] / l_ref[:, here]).astype(jnp.bfloat16)

    groups(width, body)
    if kind == "last":
        out_ref[...] = jnp.dot(att[...], w_out[...], preferred_element_type=jnp.float32).astype(jnp.bfloat16)


SMEM = pl.BlockSpec(memory_space=pltpu.SMEM)
VMEM = pl.BlockSpec(memory_space=pltpu.VMEM)


def state_shapes(width):
    return [jax.ShapeDtypeStruct((2 * BLOCK, width), jnp.float32)] * 3


def attend(gather, users, tiles, place, tele_ids, xs, w_qkv, name, q=None, state=None, w_out=None):
    kind = "first" if state is None else "step" if w_out is None else "last"
    width = xs[0].shape[-1]
    q_shape = jax.ShapeDtypeStruct((2 * BLOCK, width), jnp.bfloat16)
    out_shape = state_shapes(width)
    args = [tele_ids, *xs]
    aliases, scratch = {}, []
    if kind == "first":
        args += [w_qkv]
        out_shape = [q_shape, jax.ShapeDtypeStruct((1,) + xs[0].shape[1:], xs[0].dtype)] + out_shape
    else:
        args += [q, w_qkv] + ([w_out] if kind == "last" else []) + list(state)
        out_shape = ([q_shape] if kind == "last" else []) + out_shape
        aliases = {len(args) - 3 + k: len(out_shape) - 3 + k for k in range(3)}
        if kind == "last":
            scratch = [pltpu.VMEM((2 * BLOCK, width), jnp.bfloat16)]
    spent = tiles * COST
    return pl.pallas_call(
        functools.partial(attend_kernel, gather, users, len(xs), kind, place),
        in_specs=[SMEM] + [VMEM] * (len(args) - 1), out_specs=[VMEM] * len(out_shape), out_shape=out_shape,
        input_output_aliases=aliases, scratch_shapes=scratch, name=name,
        compiler_params=pltpu.CompilerParams(vmem_limit_bytes=VM * 1024 * 1024),
        cost_estimate=pl.CostEstimate(flops=spent, bytes_accessed=0, transcendentals=0),
    )(*args)


def gate_kernel(count, *refs):
    del count, refs


def gate(arrays, after):
    count = len(arrays)
    return pl.pallas_call(
        functools.partial(gate_kernel, count),
        in_specs=[pl.BlockSpec(memory_space=pl.ANY)] * (count + len(after)),
        out_specs=[pl.BlockSpec(memory_space=pl.ANY)] * count,
        out_shape=[jax.ShapeDtypeStruct(v.shape, v.dtype) for v in arrays],
        input_output_aliases={k: k for k in range(count)}, name="gate",
        compiler_params=pltpu.CompilerParams(vmem_limit_bytes=1024 * 1024),
    )(*arrays, *after)


PAIRS = [[0, 1], [0, 1]]
BOTH = [[0, 1, 2, 3], [0, 1, 2, 3]]


def lat_swap(array, n_lat):
    same = [(i, i ^ 1) for i in range(n_lat)]
    other = [p for i in range(1, n_lat - 1, 2) for p in ((i, i + 1), (i + 1, i))]
    return lax.ppermute(array, "lat", same), lax.ppermute(array, "lat", other)


def own_alone(at, x):
    b = 2 * at.z
    return [x[0], x[1]], [at.row(b), at.row(b + 1)]


def lon_tiles(at, near, ring_edge, ring_rest):
    odd = lax.rem(at.z, 2)
    b = 2 * (at.z + 1 - 2 * odd)
    c = 2 * lax.rem(at.z - 1 + 2 * odd + at.n_lon, at.n_lon)
    return ([near[0], near[1], ring_edge[0], ring_rest[0]],
            [at.row(b), at.row(b + 1), at.row(c + 1 - odd), at.row(c + odd)])


def across_tiles(at, far_edge, far_rest):
    odd = lax.rem(at.z, 2)
    b = 2 * lax.rem(at.z + 2, at.n_lon)
    return [far_edge[0], far_rest[0]], [at.row(b + odd), at.row(b + 1 - odd)]


def corner_tiles(at, same, other):
    return [same[0], other[0], same[1], other[1]], [at.rim(True), at.rim(False)] * 2


def rim_tiles(at, same, other):
    return [same[0], same[1], other[0], other[1]], [at.rim(True)] * 2 + [at.rim(False)] * 2


def column_tiles(start, at, row):
    found = []
    for j in range(row.shape[0]):
        own = (start + j >= 2 * at.z) & (start + j <= 2 * at.z + 1)
        found.append([jnp.where(own, jnp.float32(NEG), v) for v in at.row(jnp.int32(start + j))])
    return [row[j] for j in range(row.shape[0])], found


def on_device(tokens, w_qkv, w_out, tele_ids):
    n_lat, n_lon = lax.axis_size("lat"), lax.axis_size("lon")
    place = (n_lat, n_lon)
    z = lax.axis_index("lon")
    x = tokens[0]
    if n_lon == 4:
        near_pairs = [(i, i ^ 1) for i in range(4)]
        ring_pairs = [(0, 3), (3, 0), (1, 2), (2, 1)]
        even = lax.rem(z, 2) == 0
        near = lax.ppermute(x, "lon", near_pairs)
        ring_edge = lax.ppermute(jnp.where(even, x[:1], x[1:]), "lon", ring_pairs)
        same, other = lat_swap(x, n_lat)
        q, rest, *state = attend(own_alone, PAIRS, 3, place, tele_ids, [x], w_qkv, "own")
        ring_rest = lax.ppermute(rest, "lon", ring_pairs)
        near, ring_edge = gate([near, ring_edge], [q])
        edges = jnp.concatenate([jnp.where(even, ring_edge, near[1:]), jnp.where(even, near[:1], ring_edge)], 0)
        same_edges, other_edges = lat_swap(edges, n_lat)
        state = attend(rim_tiles, BOTH, 4, place, tele_ids, [same, other], w_qkv, "rim", q, state)
        ring_edge, ring_rest = gate([ring_edge, ring_rest], [state[1]])
        far_edge = lax.ppermute(ring_edge, "lon", near_pairs)
        far_rest = lax.ppermute(ring_rest, "lon", near_pairs)
        state = attend(lon_tiles, BOTH, 4, place, tele_ids, [near, ring_edge, ring_rest], w_qkv, "lon", q, state)
        state = attend(corner_tiles, [[0, 1], [2, 3]], 4, place, tele_ids,
                       [same_edges, other_edges], w_qkv, "corner", q, state)
        mixed = attend(across_tiles, PAIRS, 3, place, tele_ids, [far_edge, far_rest], w_qkv, "across", q, state, w_out)[0]
    else:
        q, _, *state = attend(own_alone, PAIRS, 2, place, tele_ids, [x], w_qkv, "own")
        same, other = lat_swap(x, n_lat)
        before = lax.ppermute(x[1:], "lon", [(i, (i + 1) % n_lon) for i in range(n_lon)])
        after = lax.ppermute(x[:1], "lon", [((i + 1) % n_lon, i) for i in range(n_lon)])
        same_edges, other_edges = lat_swap(jnp.concatenate([before, after], 0), n_lat)
        state = attend(rim_tiles, BOTH, 4, place, tele_ids, [same, other], w_qkv, "rim", q, state)
        state = attend(corner_tiles, [[0, 1], [2, 3]], 4, place, tele_ids,
                       [same_edges, other_edges], w_qkv, "corner", q, state)
        row = lax.all_gather(x, "lon", axis=0, tiled=True)
        for s in range(0, 2 * n_lon, 4):
            state = attend(functools.partial(column_tiles, s), BOTH, 4, place, tele_ids, [row[s:s + 4]], w_qkv,
                           "columns", q, state, w_out if s + 4 == 2 * n_lon else None)
        mixed = state[0]
    return mixed.reshape(tokens.shape)


def solution(mesh):
    return jax.shard_map(
        on_device,
        mesh=mesh,
        in_specs=(P("lat", "lon", None, None), P(), P(), P("lat", "lon", None)),
        out_specs=P("lat", "lon", None, None),
        check_vma=False,
    )
```

```python
import functools
import math
import jax
import jax.numpy as jnp
from jax import lax
from jax.experimental import pallas as pl
from jax.experimental.pallas import tpu as pltpu
from jax.sharding import PartitionSpec as P

HD = 64
BLOCK = 128
PAIR = 2 * HD
NEG = -1e30
CW = 1024
VM = 24
COST = 0
UNIT = 1.4426950408889634 * HD ** -0.5


def log_times(times):
    value = jnp.float32(NEG)
    for k in range(1, 12):
        value = jnp.where(times == k, jnp.float32(math.log(k) * HD ** 0.5), value)
    return value


def row_bias(tele_ref, own, total, column, t):
    told = jnp.int32(0)
    for k in range(tele_ref.shape[2]):
        told = told + (tele_ref[0, t, k] == column).astype(jnp.int32)
    beside = lax.rem(column - (own + t) + 1 + total, total) <= 2
    return log_times(told + beside.astype(jnp.int32))


def bias_lanes(values):
    lane = lax.broadcasted_iota(jnp.int32, (BLOCK, PAIR), 1)
    picked = jnp.zeros((BLOCK, PAIR), jnp.float32)
    for t, value in enumerate(values):
        whole = jnp.full((BLOCK, PAIR), value, jnp.float32)
        hi = whole.astype(jnp.bfloat16).astype(jnp.float32)
        mid = (whole - hi).astype(jnp.bfloat16).astype(jnp.float32)
        for k, part in enumerate((hi, mid, whole - hi - mid)):
            picked = jnp.where(lane == 3 * t + k, part, picked)
    return picked.astype(jnp.bfloat16)


def stacked(parts):
    return parts[0] if len(parts) == 1 else jnp.concatenate(parts, 0)


def update(q, keys, values, bias, users, o_ref, m_ref, l_ref, first):
    if users[0] == users[1]:
        update_some(q, keys, values, bias, users, o_ref, m_ref, l_ref, first, (0, 1))
    else:
        for t in range(2):
            update_some(q, keys, values, bias, users, o_ref, m_ref, l_ref, first, (t,))


def update_some(q, keys, values, bias, users, o_ref, m_ref, l_ref, first, which):
    lane = lax.broadcasted_iota(jnp.int32, (BLOCK, PAIR), 1)
    left = lane < HD
    picks = [((lane >= 3 * t) & (lane < 3 * t + 3)).astype(jnp.float32).astype(jnp.bfloat16) for t in range(2)]
    tiles = users[which[0]]
    lanes = [bias_lanes([bias[t][j] for t in range(2)]) for j in tiles]
    rows = [slice(t * BLOCK, (t + 1) * BLOCK) for t in range(2)]
    two = 2 * BLOCK
    for pr in range(CW // PAIR):
        cols = slice(pr * PAIR, (pr + 1) * PAIR)
        wide = []
        for t in which:
            qp = q[rows[t], cols]
            zero = jnp.zeros_like(qp)
            both = jnp.concatenate([jnp.where(left, qp, zero), jnp.where(left, zero, qp)], 0)
            wide.append(jnp.concatenate([both, jnp.concatenate([picks[t], picks[t]], 0)], 1))
        kp = stacked([jnp.concatenate([keys[j][:, cols], b], 1) for j, b in zip(tiles, lanes)])
        s = lax.dot_general(stacked(wide), kp, (((1,), (1,)), ((), ())), preferred_element_type=jnp.float32)
        peaks = jnp.max(s, axis=1, keepdims=True)
        p = jnp.exp2((s - peaks) * UNIT).astype(jnp.bfloat16)
        vp = stacked([values[j][:, cols] for j in tiles])
        vp = jnp.concatenate([vp, jnp.ones((len(tiles) * BLOCK, PAIR), jnp.bfloat16)], 1)
        sums = jnp.dot(p, vp, preferred_element_type=jnp.float32)
        for i, t in enumerate(which):
            r, m = sums[i * two:(i + 1) * two], peaks[i * two:(i + 1) * two]
            o = jnp.where(left, r[:BLOCK, :PAIR], r[BLOCK:, :PAIR])
            l = jnp.where(left, r[:BLOCK, PAIR:], r[BLOCK:, PAIR:])
            m = jnp.where(left, m[:BLOCK], m[BLOCK:])
            if not first:
                m_old = m_ref[rows[t], cols]
                peak = jnp.maximum(m, m_old)
                was = jnp.exp2((m_old - peak) * UNIT)
                now = jnp.exp2((m - peak) * UNIT)
                o = o_ref[rows[t], cols] * was + o * now
                l = l_ref[rows[t], cols] * was + l * now
                m = peak
            o_ref[rows[t], cols] = o
            l_ref[rows[t], cols] = l
            m_ref[rows[t], cols] = m


def project(xs, w, off):
    flat = jnp.concatenate(xs, 0)
    return jnp.dot(flat, w[:, pl.ds(off, CW)], preferred_element_type=jnp.float32).astype(jnp.bfloat16)


def split(a):
    return [a[i:i + BLOCK] for i in range(0, a.shape[0], BLOCK)]


def groups(width, body):
    if LOOP:
        lax.fori_loop(0, width // CW, lambda i, c: (body(pl.multiple_of(i * CW, CW)), c)[1], 0)
    else:
        for i in range(width // CW):
            body(i * CW)


LOOP = False


class Place:
    def __init__(self, tele_ref, n_lat, n_lon):
        self.tele_ref, self.n_lon = tele_ref, n_lon
        a, self.z = lax.axis_index("lat"), lax.axis_index("lon")
        self.first, self.last = self.z == 0, self.z == n_lon - 1
        self.other_ok = jnp.where(lax.rem(a, 2) == 0, a > 0, a < n_lat - 1)

    def row(self, column):
        return [row_bias(self.tele_ref, 2 * self.z, 2 * self.n_lon, column, t) for t in range(2)]

    def rim(self, same):
        value = jnp.float32(0.0) if same else jnp.where(self.other_ok, jnp.float32(0.0), jnp.float32(NEG))
        return [value, value]


def attend_kernel(gather, users, n_x, kind, place, tele_ref, *refs):
    x_refs, refs = refs[:n_x], refs[n_x:]
    at = Place(tele_ref, *place)
    xs, tiles_bias = gather(at, *x_refs)
    bias = [[both[t] for both in tiles_bias] for t in range(2)]
    width = xs[0].shape[-1]
    if kind == "first":
        w, q_ref, o_ref, m_ref, l_ref = refs
    elif kind == "last":
        q_ref, w, w_out, o_in, m_in, l_in, out_ref, o_ref, m_ref, l_ref, att = refs
    else:
        q_ref, w, o_in, m_in, l_in, o_ref, m_ref, l_ref = refs

    def body(off):
        here = pl.ds(off, CW)
        if kind == "first":
            q = project(xs[:2], w, off)
            q_ref[:, here] = q
        else:
            q = q_ref[:, here]
        keys, values = split(project(xs, w, width + off)), split(project(xs, w, 2 * width + off))
        update(q, keys, values, bias, users, o_ref.at[:, here], m_ref.at[:, here], l_ref.at[:, here], kind == "first")
        if kind == "last":
            att[:, here] = (o_ref[:, here] / l_ref[:, here]).astype(jnp.bfloat16)

    groups(width, body)
    if kind == "last":
        out_ref[...] = jnp.dot(att[...], w_out[...], preferred_element_type=jnp.float32).astype(jnp.bfloat16)


SMEM = pl.BlockSpec(memory_space=pltpu.SMEM)
VMEM = pl.BlockSpec(memory_space=pltpu.VMEM)


def state_shapes(width):
    return [jax.ShapeDtypeStruct((2 * BLOCK, width), jnp.float32)] * 3


def attend(gather, users, tiles, place, tele_ids, xs, w_qkv, name, q=None, state=None, w_out=None):
    kind = "first" if state is None else "step" if w_out is None else "last"
    width = xs[0].shape[-1]
    q_shape = jax.ShapeDtypeStruct((2 * BLOCK, width), jnp.bfloat16)
    out_shape = state_shapes(width)
    args = [tele_ids, *xs]
    aliases, scratch = {}, []
    if kind == "first":
        args += [w_qkv]
        out_shape = [q_shape] + out_shape
    else:
        args += [q, w_qkv] + ([w_out] if kind == "last" else []) + list(state)
        out_shape = ([q_shape] if kind == "last" else []) + out_shape
        aliases = {len(args) - 3 + k: len(out_shape) - 3 + k for k in range(3)}
        if kind == "last":
            scratch = [pltpu.VMEM((2 * BLOCK, width), jnp.bfloat16)]
    spent = tiles * COST
    return pl.pallas_call(
        functools.partial(attend_kernel, gather, users, len(xs), kind, place),
        in_specs=[SMEM] + [VMEM] * (len(args) - 1), out_specs=[VMEM] * len(out_shape), out_shape=out_shape,
        input_output_aliases=aliases, scratch_shapes=scratch, name=name,
        compiler_params=pltpu.CompilerParams(vmem_limit_bytes=VM * 1024 * 1024),
        cost_estimate=pl.CostEstimate(flops=spent, bytes_accessed=0, transcendentals=0),
    )(*args)


def gate_kernel(count, *refs):
    del count, refs


def gate(arrays, after):
    count = len(arrays)
    return pl.pallas_call(
        functools.partial(gate_kernel, count),
        in_specs=[pl.BlockSpec(memory_space=pl.ANY)] * (count + len(after)),
        out_specs=[pl.BlockSpec(memory_space=pl.ANY)] * count,
        out_shape=[jax.ShapeDtypeStruct(v.shape, v.dtype) for v in arrays],
        input_output_aliases={k: k for k in range(count)}, name="gate",
        compiler_params=pltpu.CompilerParams(vmem_limit_bytes=1024 * 1024),
    )(*arrays, *after)


PAIRS = [[0, 1], [0, 1]]
BOTH = [[0, 1, 2, 3], [0, 1, 2, 3]]


def lat_swap(array, n_lat):
    same = [(i, i ^ 1) for i in range(n_lat)]
    other = [p for i in range(1, n_lat - 1, 2) for p in ((i, i + 1), (i + 1, i))]
    return lax.ppermute(array, "lat", same), lax.ppermute(array, "lat", other)


def own_alone(at, x):
    b = 2 * at.z
    return [x[0], x[1]], [at.row(b), at.row(b + 1)]


def lon_tiles(at, near_edge, near_rest, ring_edge, ring_rest):
    odd = lax.rem(at.z, 2)
    b = 2 * (at.z + 1 - 2 * odd)
    c = 2 * lax.rem(at.z - 1 + 2 * odd + at.n_lon, at.n_lon)
    return ([near_edge[0], near_rest[0], ring_edge[0], ring_rest[0]],
            [at.row(b + odd), at.row(b + 1 - odd), at.row(c + 1 - odd), at.row(c + odd)])


def across_tiles(at, far_edge, far_rest):
    odd = lax.rem(at.z, 2)
    b = 2 * lax.rem(at.z + 2, at.n_lon)
    return [far_edge[0], far_rest[0]], [at.row(b + odd), at.row(b + 1 - odd)]


def corner_tiles(at, same, other):
    return [same[0], other[0], same[1], other[1]], [at.rim(True), at.rim(False)] * 2


def rim_tiles(at, same, other):
    return [same[0], same[1], other[0], other[1]], [at.rim(True)] * 2 + [at.rim(False)] * 2


def column_tiles(start, at, row):
    found = []
    for j in range(row.shape[0]):
        own = (start + j >= 2 * at.z) & (start + j <= 2 * at.z + 1)
        found.append([jnp.where(own, jnp.float32(NEG), v) for v in at.row(jnp.int32(start + j))])
    return [row[j] for j in range(row.shape[0])], found


def on_device(tokens, w_qkv, w_out, tele_ids):
    n_lat, n_lon = lax.axis_size("lat"), lax.axis_size("lon")
    place = (n_lat, n_lon)
    z = lax.axis_index("lon")
    x = tokens[0]
    if n_lon == 4:
        near_pairs = [(i, i ^ 1) for i in range(4)]
        ring_pairs = [(0, 3), (3, 0), (1, 2), (2, 1)]
        even = lax.rem(z, 2) == 0
        inner, outer = jnp.where(even, x[1:], x[:1]), jnp.where(even, x[:1], x[1:])
        near_edge = lax.ppermute(inner, "lon", near_pairs)
        ring_edge = lax.ppermute(outer, "lon", ring_pairs)
        same, other = lat_swap(x, n_lat)
        q, *state = attend(own_alone, PAIRS, 3, place, tele_ids, [x], w_qkv, "own")
        near_rest = lax.ppermute(outer, "lon", near_pairs)
        ring_rest = lax.ppermute(inner, "lon", ring_pairs)
        near_edge, ring_edge = gate([near_edge, ring_edge], [q])
        edges = jnp.concatenate([jnp.where(even, ring_edge, near_edge), jnp.where(even, near_edge, ring_edge)], 0)
        same_edges, other_edges = lat_swap(edges, n_lat)
        state = attend(rim_tiles, BOTH, 4, place, tele_ids, [same, other], w_qkv, "rim", q, state)
        ring_edge, ring_rest, near_rest = gate([ring_edge, ring_rest, near_rest], [state[1]])
        far_edge = lax.ppermute(ring_edge, "lon", near_pairs)
        far_rest = lax.ppermute(ring_rest, "lon", near_pairs)
        state = attend(lon_tiles, BOTH, 4, place, tele_ids, [near_edge, near_rest, ring_edge, ring_rest], w_qkv, "lon", q, state)
        state = attend(corner_tiles, [[0, 1], [2, 3]], 4, place, tele_ids,
                       [same_edges, other_edges], w_qkv, "corner", q, state)
        mixed = attend(across_tiles, PAIRS, 3, place, tele_ids, [far_edge, far_rest], w_qkv, "across", q, state, w_out)[0]
    else:
        q, *state = attend(own_alone, PAIRS, 2, place, tele_ids, [x], w_qkv, "own")
        same, other = lat_swap(x, n_lat)
        before = lax.ppermute(x[1:], "lon", [(i, (i + 1) % n_lon) for i in range(n_lon)])
        after = lax.ppermute(x[:1], "lon", [((i + 1) % n_lon, i) for i in range(n_lon)])
        same_edges, other_edges = lat_swap(jnp.concatenate([before, after], 0), n_lat)
        state = attend(rim_tiles, BOTH, 4, place, tele_ids, [same, other], w_qkv, "rim", q, state)
        state = attend(corner_tiles, [[0, 1], [2, 3]], 4, place, tele_ids,
                       [same_edges, other_edges], w_qkv, "corner", q, state)
        row = lax.all_gather(x, "lon", axis=0, tiled=True)
        for s in range(0, 2 * n_lon, 4):
            state = attend(functools.partial(column_tiles, s), BOTH, 4, place, tele_ids, [row[s:s + 4]], w_qkv,
                           "columns", q, state, w_out if s + 4 == 2 * n_lon else None)
        mixed = state[0]
    return mixed.reshape(tokens.shape)


def solution(mesh):
    return jax.shard_map(
        on_device,
        mesh=mesh,
        in_specs=(P("lat", "lon", None, None), P(), P(), P("lat", "lon", None)),
        out_specs=P("lat", "lon", None, None),
        check_vma=False,
    )
```

```python
import functools
import math
import jax
import jax.numpy as jnp
from jax import lax
from jax.experimental import pallas as pl
from jax.experimental.pallas import tpu as pltpu
from jax.sharding import PartitionSpec as P

HD = 64
BLOCK = 128
PAIR = 2 * HD
NEG = -1e30
CW = 1024
VM = 24
FIRST_VM = 46
COST = 0
UNIT = 1.4426950408889634 * HD ** -0.5


def log_times(times):
    value = jnp.float32(NEG)
    for k in range(1, 12):
        value = jnp.where(times == k, jnp.float32(math.log(k) * HD ** 0.5), value)
    return value


def row_bias(tele_ref, own, total, column, t):
    told = jnp.int32(0)
    for k in range(tele_ref.shape[2]):
        told = told + (tele_ref[0, t, k] == column).astype(jnp.int32)
    beside = lax.rem(column - (own + t) + 1 + total, total) <= 2
    return log_times(told + beside.astype(jnp.int32))


def bias_lanes(values):
    lane = lax.broadcasted_iota(jnp.int32, (BLOCK, PAIR), 1)
    picked = jnp.zeros((BLOCK, PAIR), jnp.float32)
    for t, value in enumerate(values):
        whole = jnp.full((BLOCK, PAIR), value, jnp.float32)
        hi = whole.astype(jnp.bfloat16).astype(jnp.float32)
        mid = (whole - hi).astype(jnp.bfloat16).astype(jnp.float32)
        for k, part in enumerate((hi, mid, whole - hi - mid)):
            picked = jnp.where(lane == 3 * t + k, part, picked)
    return picked.astype(jnp.bfloat16)


def stacked(parts):
    return parts[0] if len(parts) == 1 else jnp.concatenate(parts, 0)


def update(q, keys, values, bias, users, o_ref, m_ref, l_ref, first):
    if users[0] == users[1]:
        update_some(q, keys, values, bias, users, o_ref, m_ref, l_ref, first, (0, 1))
    else:
        for t in range(2):
            update_some(q, keys, values, bias, users, o_ref, m_ref, l_ref, first, (t,))


def update_some(q, keys, values, bias, users, o_ref, m_ref, l_ref, first, which):
    lane = lax.broadcasted_iota(jnp.int32, (BLOCK, PAIR), 1)
    left = lane < HD
    picks = [((lane >= 3 * t) & (lane < 3 * t + 3)).astype(jnp.float32).astype(jnp.bfloat16) for t in range(2)]
    tiles = users[which[0]]
    lanes = [bias_lanes([bias[t][j] for t in range(2)]) for j in tiles]
    rows = [slice(t * BLOCK, (t + 1) * BLOCK) for t in range(2)]
    two = 2 * BLOCK
    for pr in range(CW // PAIR):
        cols = slice(pr * PAIR, (pr + 1) * PAIR)
        wide = []
        for t in which:
            qp = q[rows[t], cols]
            zero = jnp.zeros_like(qp)
            both = jnp.concatenate([jnp.where(left, qp, zero), jnp.where(left, zero, qp)], 0)
            wide.append(jnp.concatenate([both, jnp.concatenate([picks[t], picks[t]], 0)], 1))
        kp = stacked([jnp.concatenate([keys[j][:, cols], b], 1) for j, b in zip(tiles, lanes)])
        s = lax.dot_general(stacked(wide), kp, (((1,), (1,)), ((), ())), preferred_element_type=jnp.float32)
        peaks = jnp.max(s, axis=1, keepdims=True)
        p = jnp.exp2((s - peaks) * UNIT).astype(jnp.bfloat16)
        vp = stacked([values[j][:, cols] for j in tiles])
        vp = jnp.concatenate([vp, jnp.ones((len(tiles) * BLOCK, PAIR), jnp.bfloat16)], 1)
        sums = jnp.dot(p, vp, preferred_element_type=jnp.float32)
        for i, t in enumerate(which):
            r, m = sums[i * two:(i + 1) * two], peaks[i * two:(i + 1) * two]
            o = jnp.where(left, r[:BLOCK, :PAIR], r[BLOCK:, :PAIR])
            l = jnp.where(left, r[:BLOCK, PAIR:], r[BLOCK:, PAIR:])
            m = jnp.where(left, m[:BLOCK], m[BLOCK:])
            if not first:
                m_old = m_ref[rows[t], cols]
                peak = jnp.maximum(m, m_old)
                was = jnp.exp2((m_old - peak) * UNIT)
                now = jnp.exp2((m - peak) * UNIT)
                o = o_ref[rows[t], cols] * was + o * now
                l = l_ref[rows[t], cols] * was + l * now
                m = peak
            o_ref[rows[t], cols] = o
            l_ref[rows[t], cols] = l
            m_ref[rows[t], cols] = m


def project(xs, w, off):
    flat = jnp.concatenate(xs, 0)
    return jnp.dot(flat, w[:, pl.ds(off, CW)], preferred_element_type=jnp.float32).astype(jnp.bfloat16)


def split(a):
    return [a[i:i + BLOCK] for i in range(0, a.shape[0], BLOCK)]


def groups(width, body):
    if LOOP:
        lax.fori_loop(0, width // CW, lambda i, c: (body(pl.multiple_of(i * CW, CW)), c)[1], 0)
    else:
        for i in range(width // CW):
            body(i * CW)


LOOP = False


class Place:
    def __init__(self, tele_ref, n_lat, n_lon):
        self.tele_ref, self.n_lon = tele_ref, n_lon
        a, self.z = lax.axis_index("lat"), lax.axis_index("lon")
        self.first, self.last = self.z == 0, self.z == n_lon - 1
        self.other_ok = jnp.where(lax.rem(a, 2) == 0, a > 0, a < n_lat - 1)

    def row(self, column):
        return [row_bias(self.tele_ref, 2 * self.z, 2 * self.n_lon, column, t) for t in range(2)]

    def rim(self, same):
        value = jnp.float32(0.0) if same else jnp.where(self.other_ok, jnp.float32(0.0), jnp.float32(NEG))
        return [value, value]


def attend_kernel(gather, users, n_x, kind, place, tele_ref, *refs):
    x_refs, refs = refs[:n_x], refs[n_x:]
    at = Place(tele_ref, *place)
    xs, tiles_bias = gather(at, *x_refs)
    bias = [[both[t] for both in tiles_bias] for t in range(2)]
    width = xs[0].shape[-1]
    if kind == "first":
        w, q_ref, o_ref, m_ref, l_ref = refs
    elif kind == "last":
        q_ref, w, w_out, o_in, m_in, l_in, out_ref, o_ref, m_ref, l_ref, att = refs
    else:
        q_ref, w, o_in, m_in, l_in, o_ref, m_ref, l_ref = refs

    def body(off):
        here = pl.ds(off, CW)
        if kind == "first":
            q = project(xs[:2], w, off)
            q_ref[:, here] = q
        else:
            q = q_ref[:, here]
        keys, values = split(project(xs, w, width + off)), split(project(xs, w, 2 * width + off))
        update(q, keys, values, bias, users, o_ref.at[:, here], m_ref.at[:, here], l_ref.at[:, here], kind == "first")
        if kind == "last":
            att[:, here] = (o_ref[:, here] / l_ref[:, here]).astype(jnp.bfloat16)

    groups(width, body)
    if kind == "last":
        out_ref[...] = jnp.dot(att[...], w_out[...], preferred_element_type=jnp.float32).astype(jnp.bfloat16)


SMEM = pl.BlockSpec(memory_space=pltpu.SMEM)
VMEM = pl.BlockSpec(memory_space=pltpu.VMEM)


def state_shapes(width):
    return [jax.ShapeDtypeStruct((2 * BLOCK, width), jnp.float32)] * 3


def attend(gather, users, tiles, place, tele_ids, xs, w_qkv, name, q=None, state=None, w_out=None):
    kind = "first" if state is None else "step" if w_out is None else "last"
    width = xs[0].shape[-1]
    q_shape = jax.ShapeDtypeStruct((2 * BLOCK, width), jnp.bfloat16)
    out_shape = state_shapes(width)
    args = [tele_ids, *xs]
    aliases, scratch = {}, []
    if kind == "first":
        args += [w_qkv]
        out_shape = [q_shape] + out_shape
    else:
        args += [q, w_qkv] + ([w_out] if kind == "last" else []) + list(state)
        out_shape = ([q_shape] if kind == "last" else []) + out_shape
        aliases = {len(args) - 3 + k: len(out_shape) - 3 + k for k in range(3)}
        if kind == "last":
            scratch = [pltpu.VMEM((2 * BLOCK, width), jnp.bfloat16)]
    spent = tiles * COST
    return pl.pallas_call(
        functools.partial(attend_kernel, gather, users, len(xs), kind, place),
        in_specs=[SMEM] + [VMEM] * (len(args) - 1), out_specs=[VMEM] * len(out_shape), out_shape=out_shape,
        input_output_aliases=aliases, scratch_shapes=scratch, name=name,
        compiler_params=pltpu.CompilerParams(vmem_limit_bytes=(FIRST_VM if kind == "first" else VM) * 1024 * 1024),
        cost_estimate=pl.CostEstimate(flops=spent, bytes_accessed=0, transcendentals=0),
    )(*args)


def gate_kernel(count, *refs):
    del count, refs


def gate(arrays, after):
    count = len(arrays)
    return pl.pallas_call(
        functools.partial(gate_kernel, count),
        in_specs=[pl.BlockSpec(memory_space=pl.ANY)] * (count + len(after)),
        out_specs=[pl.BlockSpec(memory_space=pl.ANY)] * count,
        out_shape=[jax.ShapeDtypeStruct(v.shape, v.dtype) for v in arrays],
        input_output_aliases={k: k for k in range(count)}, name="gate",
        compiler_params=pltpu.CompilerParams(vmem_limit_bytes=1024 * 1024),
    )(*arrays, *after)


PAIRS = [[0, 1], [0, 1]]
BOTH = [[0, 1, 2, 3], [0, 1, 2, 3]]


def lat_swap(array, n_lat):
    same = [(i, i ^ 1) for i in range(n_lat)]
    other = [p for i in range(1, n_lat - 1, 2) for p in ((i, i + 1), (i + 1, i))]
    return lax.ppermute(array, "lat", same), lax.ppermute(array, "lat", other)


def own_alone(at, x):
    b = 2 * at.z
    return [x[0], x[1]], [at.row(b), at.row(b + 1)]


def lon_tiles(at, near_edge, near_rest, ring_edge, ring_rest):
    odd = lax.rem(at.z, 2)
    b = 2 * (at.z + 1 - 2 * odd)
    c = 2 * lax.rem(at.z - 1 + 2 * odd + at.n_lon, at.n_lon)
    return ([near_edge[0], near_rest[0], ring_edge[0], ring_rest[0]],
            [at.row(b + odd), at.row(b + 1 - odd), at.row(c + 1 - odd), at.row(c + odd)])


def across_tiles(at, far_edge, far_rest):
    odd = lax.rem(at.z, 2)
    b = 2 * lax.rem(at.z + 2, at.n_lon)
    return [far_edge[0], far_rest[0]], [at.row(b + odd), at.row(b + 1 - odd)]


def corner_tiles(at, same, other):
    return [same[0], other[0], same[1], other[1]], [at.rim(True), at.rim(False)] * 2


def rim_tiles(at, same, other):
    return [same[0], same[1], other[0], other[1]], [at.rim(True)] * 2 + [at.rim(False)] * 2


def column_tiles(start, at, row):
    found = []
    for j in range(row.shape[0]):
        own = (start + j >= 2 * at.z) & (start + j <= 2 * at.z + 1)
        found.append([jnp.where(own, jnp.float32(NEG), v) for v in at.row(jnp.int32(start + j))])
    return [row[j] for j in range(row.shape[0])], found


def on_device(tokens, w_qkv, w_out, tele_ids):
    n_lat, n_lon = lax.axis_size("lat"), lax.axis_size("lon")
    place = (n_lat, n_lon)
    z = lax.axis_index("lon")
    x = tokens[0]
    if n_lon == 4:
        near_pairs = [(i, i ^ 1) for i in range(4)]
        ring_pairs = [(0, 3), (3, 0), (1, 2), (2, 1)]
        even = lax.rem(z, 2) == 0
        inner, outer = jnp.where(even, x[1:], x[:1]), jnp.where(even, x[:1], x[1:])
        near_edge = lax.ppermute(inner, "lon", near_pairs)
        ring_edge = lax.ppermute(outer, "lon", ring_pairs)
        same, other = lat_swap(x, n_lat)
        q, *state = attend(own_alone, PAIRS, 3, place, tele_ids, [x], w_qkv, "own")
        near_rest = lax.ppermute(outer, "lon", near_pairs)
        ring_rest = lax.ppermute(inner, "lon", ring_pairs)
        near_edge, ring_edge = gate([near_edge, ring_edge], [q])
        edges = jnp.concatenate([jnp.where(even, ring_edge, near_edge), jnp.where(even, near_edge, ring_edge)], 0)
        same_edges, other_edges = lat_swap(edges, n_lat)
        state = attend(rim_tiles, BOTH, 4, place, tele_ids, [same, other], w_qkv, "rim", q, state)
        ring_edge, ring_rest, near_rest = gate([ring_edge, ring_rest, near_rest], [state[1]])
        far_edge = lax.ppermute(ring_edge, "lon", near_pairs)
        far_rest = lax.ppermute(ring_rest, "lon", near_pairs)
        state = attend(lon_tiles, BOTH, 4, place, tele_ids, [near_edge, near_rest, ring_edge, ring_rest], w_qkv, "lon", q, state)
        state = attend(corner_tiles, [[0, 1], [2, 3]], 4, place, tele_ids,
                       [same_edges, other_edges], w_qkv, "corner", q, state)
        mixed = attend(across_tiles, PAIRS, 3, place, tele_ids, [far_edge, far_rest], w_qkv, "across", q, state, w_out)[0]
    else:
        q, *state = attend(own_alone, PAIRS, 2, place, tele_ids, [x], w_qkv, "own")
        same, other = lat_swap(x, n_lat)
        before = lax.ppermute(x[1:], "lon", [(i, (i + 1) % n_lon) for i in range(n_lon)])
        after = lax.ppermute(x[:1], "lon", [((i + 1) % n_lon, i) for i in range(n_lon)])
        same_edges, other_edges = lat_swap(jnp.concatenate([before, after], 0), n_lat)
        state = attend(rim_tiles, BOTH, 4, place, tele_ids, [same, other], w_qkv, "rim", q, state)
        state = attend(corner_tiles, [[0, 1], [2, 3]], 4, place, tele_ids,
                       [same_edges, other_edges], w_qkv, "corner", q, state)
        row = lax.all_gather(x, "lon", axis=0, tiled=True)
        for s in range(0, 2 * n_lon, 4):
            state = attend(functools.partial(column_tiles, s), BOTH, 4, place, tele_ids, [row[s:s + 4]], w_qkv,
                           "columns", q, state, w_out if s + 4 == 2 * n_lon else None)
        mixed = state[0]
    return mixed.reshape(tokens.shape)


def solution(mesh):
    return jax.shard_map(
        on_device,
        mesh=mesh,
        in_specs=(P("lat", "lon", None, None), P(), P(), P("lat", "lon", None)),
        out_specs=P("lat", "lon", None, None),
        check_vma=False,
    )
```

```python
import functools
import math
import jax
import jax.numpy as jnp
from jax import lax
from jax.experimental import pallas as pl
from jax.experimental.pallas import tpu as pltpu
from jax.sharding import PartitionSpec as P

HD = 64
BLOCK = 128
PAIR = 2 * HD
NEG = -1e30
CW = 1024
VM = 24
FIRST_VM = 46
COST = 0
UNIT = 1.4426950408889634 * HD ** -0.5


def log_times(times):
    value = jnp.float32(NEG)
    for k in range(1, 12):
        value = jnp.where(times == k, jnp.float32(math.log(k) * HD ** 0.5), value)
    return value


def row_bias(tele_ref, own, total, column, t):
    told = jnp.int32(0)
    for k in range(tele_ref.shape[2]):
        told = told + (tele_ref[0, t, k] == column).astype(jnp.int32)
    beside = lax.rem(column - (own + t) + 1 + total, total) <= 2
    return log_times(told + beside.astype(jnp.int32))


def bias_lanes(values):
    lane = lax.broadcasted_iota(jnp.int32, (BLOCK, PAIR), 1)
    picked = jnp.zeros((BLOCK, PAIR), jnp.float32)
    for t, value in enumerate(values):
        whole = jnp.full((BLOCK, PAIR), value, jnp.float32)
        hi = whole.astype(jnp.bfloat16).astype(jnp.float32)
        mid = (whole - hi).astype(jnp.bfloat16).astype(jnp.float32)
        for k, part in enumerate((hi, mid, whole - hi - mid)):
            picked = jnp.where(lane == 3 * t + k, part, picked)
    return picked.astype(jnp.bfloat16)


def stacked(parts):
    return parts[0] if len(parts) == 1 else jnp.concatenate(parts, 0)


def update(q, keys, values, bias, users, o_ref, m_ref, l_ref, first):
    if users[0] == users[1]:
        update_some(q, keys, values, bias, users, o_ref, m_ref, l_ref, first, (0, 1))
    else:
        for t in range(2):
            update_some(q, keys, values, bias, users, o_ref, m_ref, l_ref, first, (t,))


def update_some(q, keys, values, bias, users, o_ref, m_ref, l_ref, first, which):
    lane = lax.broadcasted_iota(jnp.int32, (BLOCK, PAIR), 1)
    left = lane < HD
    picks = [((lane >= 3 * t) & (lane < 3 * t + 3)).astype(jnp.float32).astype(jnp.bfloat16) for t in range(2)]
    tiles = users[which[0]]
    lanes = [bias_lanes([bias[t][j] for t in range(2)]) for j in tiles]
    rows = [slice(t * BLOCK, (t + 1) * BLOCK) for t in range(2)]
    two = 2 * BLOCK
    for pr in range(CW // PAIR):
        cols = slice(pr * PAIR, (pr + 1) * PAIR)
        wide = []
        for t in which:
            qp = q[rows[t], cols]
            zero = jnp.zeros_like(qp)
            both = jnp.concatenate([jnp.where(left, qp, zero), jnp.where(left, zero, qp)], 0)
            wide.append(jnp.concatenate([both, jnp.concatenate([picks[t], picks[t]], 0)], 1))
        kp = stacked([jnp.concatenate([keys[j][:, cols], b], 1) for j, b in zip(tiles, lanes)])
        s = lax.dot_general(stacked(wide), kp, (((1,), (1,)), ((), ())), preferred_element_type=jnp.float32)
        peaks = jnp.max(s, axis=1, keepdims=True)
        p = jnp.exp2((s - peaks) * UNIT).astype(jnp.bfloat16)
        vp = stacked([values[j][:, cols] for j in tiles])
        vp = jnp.concatenate([vp, jnp.ones((len(tiles) * BLOCK, PAIR), jnp.bfloat16)], 1)
        sums = jnp.dot(p, vp, preferred_element_type=jnp.float32)
        for i, t in enumerate(which):
            r, m = sums[i * two:(i + 1) * two], peaks[i * two:(i + 1) * two]
            o = jnp.where(left, r[:BLOCK, :PAIR], r[BLOCK:, :PAIR])
            l = jnp.where(left, r[:BLOCK, PAIR:], r[BLOCK:, PAIR:])
            m = jnp.where(left, m[:BLOCK], m[BLOCK:])
            if not first:
                m_old = m_ref[rows[t], cols]
                peak = jnp.maximum(m, m_old)
                was = jnp.exp2((m_old - peak) * UNIT)
                now = jnp.exp2((m - peak) * UNIT)
                o = o_ref[rows[t], cols] * was + o * now
                l = l_ref[rows[t], cols] * was + l * now
                m = peak
            o_ref[rows[t], cols] = o
            l_ref[rows[t], cols] = l
            m_ref[rows[t], cols] = m


def project(xs, w, off):
    flat = jnp.concatenate(xs, 0)
    return jnp.dot(flat, w[:, pl.ds(off, CW)], preferred_element_type=jnp.float32).astype(jnp.bfloat16)


def split(a):
    return [a[i:i + BLOCK] for i in range(0, a.shape[0], BLOCK)]


def groups(width, body):
    if LOOP:
        lax.fori_loop(0, width // CW, lambda i, c: (body(pl.multiple_of(i * CW, CW)), c)[1], 0)
    else:
        for i in range(width // CW):
            body(i * CW)


LOOP = False


class Place:
    def __init__(self, tele_ref, n_lat, n_lon):
        self.tele_ref, self.n_lon = tele_ref, n_lon
        a, self.z = lax.axis_index("lat"), lax.axis_index("lon")
        self.first, self.last = self.z == 0, self.z == n_lon - 1
        self.other_ok = jnp.where(lax.rem(a, 2) == 0, a > 0, a < n_lat - 1)

    def row(self, column):
        return [row_bias(self.tele_ref, 2 * self.z, 2 * self.n_lon, column, t) for t in range(2)]

    def rim(self, same):
        value = jnp.float32(0.0) if same else jnp.where(self.other_ok, jnp.float32(0.0), jnp.float32(NEG))
        return [value, value]


def attend_kernel(gather, users, n_x, kind, place, tele_ref, *refs):
    x_refs, refs = refs[:n_x], refs[n_x:]
    at = Place(tele_ref, *place)
    xs, tiles_bias = gather(at, *x_refs)
    bias = [[both[t] for both in tiles_bias] for t in range(2)]
    width = xs[0].shape[-1]
    if kind == "first":
        w, q_ref, o_ref, m_ref, l_ref = refs
    elif kind == "last":
        q_ref, w, w_out, o_in, m_in, l_in, out_ref, o_ref, m_ref, l_ref, att, mixed, out_sems = refs
    else:
        q_ref, w, o_in, m_in, l_in, o_ref, m_ref, l_ref = refs

    def body(off):
        here = pl.ds(off, CW)
        if kind == "first":
            q = project(xs[:2], w, off)
            q_ref[:, here] = q
        else:
            q = q_ref[:, here]
        keys, values = split(project(xs, w, width + off)), split(project(xs, w, 2 * width + off))
        update(q, keys, values, bias, users, o_ref.at[:, here], m_ref.at[:, here], l_ref.at[:, here], kind == "first")
        if kind == "last":
            att[:, here] = (o_ref[:, here] / l_ref[:, here]).astype(jnp.bfloat16)

    groups(width, body)
    if kind == "last":
        copies = []
        for k in range(2):
            part = slice(k * width // 2, (k + 1) * width // 2)
            mixed[:, part] = jnp.dot(att[...], w_out[:, part], preferred_element_type=jnp.float32).astype(jnp.bfloat16)
            copies.append(pltpu.make_async_copy(mixed.at[:, part], out_ref.at[:, part], out_sems.at[k]))
            copies[k].start()
        for copy in copies:
            copy.wait()


SMEM = pl.BlockSpec(memory_space=pltpu.SMEM)
VMEM = pl.BlockSpec(memory_space=pltpu.VMEM)


def state_shapes(width):
    return [jax.ShapeDtypeStruct((2 * BLOCK, width), jnp.float32)] * 3


def attend(gather, users, tiles, place, tele_ids, xs, w_qkv, name, q=None, state=None, w_out=None):
    kind = "first" if state is None else "step" if w_out is None else "last"
    width = xs[0].shape[-1]
    q_shape = jax.ShapeDtypeStruct((2 * BLOCK, width), jnp.bfloat16)
    out_shape = state_shapes(width)
    args = [tele_ids, *xs]
    aliases, scratch = {}, []
    if kind == "first":
        args += [w_qkv]
        out_shape = [q_shape] + out_shape
    else:
        args += [q, w_qkv] + ([w_out] if kind == "last" else []) + list(state)
        out_shape = ([q_shape] if kind == "last" else []) + out_shape
        aliases = {len(args) - 3 + k: len(out_shape) - 3 + k for k in range(3)}
        if kind == "last":
            scratch = [pltpu.VMEM((2 * BLOCK, width), jnp.bfloat16)] * 2 + [pltpu.SemaphoreType.DMA((2,))]
    spent = tiles * COST
    return pl.pallas_call(
        functools.partial(attend_kernel, gather, users, len(xs), kind, place),
        in_specs=[SMEM] + [VMEM] * (len(args) - 1), out_specs=([pl.BlockSpec(memory_space=pl.ANY)] if kind == "last" else [VMEM]) + [VMEM] * (len(out_shape) - 1), out_shape=out_shape,
        input_output_aliases=aliases, scratch_shapes=scratch, name=name,
        compiler_params=pltpu.CompilerParams(vmem_limit_bytes=(FIRST_VM if kind == "first" else VM) * 1024 * 1024),
        cost_estimate=pl.CostEstimate(flops=spent, bytes_accessed=0, transcendentals=0),
    )(*args)


def gate_kernel(count, *refs):
    del count, refs


def gate(arrays, after):
    count = len(arrays)
    return pl.pallas_call(
        functools.partial(gate_kernel, count),
        in_specs=[pl.BlockSpec(memory_space=pl.ANY)] * (count + len(after)),
        out_specs=[pl.BlockSpec(memory_space=pl.ANY)] * count,
        out_shape=[jax.ShapeDtypeStruct(v.shape, v.dtype) for v in arrays],
        input_output_aliases={k: k for k in range(count)}, name="gate",
        compiler_params=pltpu.CompilerParams(vmem_limit_bytes=1024 * 1024),
    )(*arrays, *after)


PAIRS = [[0, 1], [0, 1]]
BOTH = [[0, 1, 2, 3], [0, 1, 2, 3]]


def lat_swap(array, n_lat):
    same = [(i, i ^ 1) for i in range(n_lat)]
    other = [p for i in range(1, n_lat - 1, 2) for p in ((i, i + 1), (i + 1, i))]
    return lax.ppermute(array, "lat", same), lax.ppermute(array, "lat", other)


def own_alone(at, x):
    b = 2 * at.z
    return [x[0], x[1]], [at.row(b), at.row(b + 1)]


def lon_tiles(at, near_edge, near_rest, ring_edge, ring_rest):
    odd = lax.rem(at.z, 2)
    b = 2 * (at.z + 1 - 2 * odd)
    c = 2 * lax.rem(at.z - 1 + 2 * odd + at.n_lon, at.n_lon)
    return ([near_edge[0], near_rest[0], ring_edge[0], ring_rest[0]],
            [at.row(b + odd), at.row(b + 1 - odd), at.row(c + 1 - odd), at.row(c + odd)])


def across_tiles(at, far_edge, far_rest):
    odd = lax.rem(at.z, 2)
    b = 2 * lax.rem(at.z + 2, at.n_lon)
    return [far_edge[0], far_rest[0]], [at.row(b + odd), at.row(b + 1 - odd)]


def corner_tiles(at, same, other):
    return [same[0], other[0], same[1], other[1]], [at.rim(True), at.rim(False)] * 2


def rim_tiles(at, same, other):
    return [same[0], same[1], other[0], other[1]], [at.rim(True)] * 2 + [at.rim(False)] * 2


def column_tiles(start, at, row):
    found = []
    for j in range(row.shape[0]):
        own = (start + j >= 2 * at.z) & (start + j <= 2 * at.z + 1)
        found.append([jnp.where(own, jnp.float32(NEG), v) for v in at.row(jnp.int32(start + j))])
    return [row[j] for j in range(row.shape[0])], found


def on_device(tokens, w_qkv, w_out, tele_ids):
    n_lat, n_lon = lax.axis_size("lat"), lax.axis_size("lon")
    place = (n_lat, n_lon)
    z = lax.axis_index("lon")
    x = tokens[0]
    if n_lon == 4:
        near_pairs = [(i, i ^ 1) for i in range(4)]
        ring_pairs = [(0, 3), (3, 0), (1, 2), (2, 1)]
        even = lax.rem(z, 2) == 0
        inner, outer = jnp.where(even, x[1:], x[:1]), jnp.where(even, x[:1], x[1:])
        near_edge = lax.ppermute(inner, "lon", near_pairs)
        ring_edge = lax.ppermute(outer, "lon", ring_pairs)
        same, other = lat_swap(x, n_lat)
        q, *state = attend(own_alone, PAIRS, 3, place, tele_ids, [x], w_qkv, "own")
        near_rest = lax.ppermute(outer, "lon", near_pairs)
        ring_rest = lax.ppermute(inner, "lon", ring_pairs)
        near_edge, ring_edge = gate([near_edge, ring_edge], [q])
        edges = jnp.concatenate([jnp.where(even, ring_edge, near_edge), jnp.where(even, near_edge, ring_edge)], 0)
        same_edges, other_edges = lat_swap(edges, n_lat)
        state = attend(rim_tiles, BOTH, 4, place, tele_ids, [same, other], w_qkv, "rim", q, state)
        ring_edge, ring_rest, near_rest = gate([ring_edge, ring_rest, near_rest], [state[1]])
        far_edge = lax.ppermute(ring_edge, "lon", near_pairs)
        far_rest = lax.ppermute(ring_rest, "lon", near_pairs)
        state = attend(lon_tiles, BOTH, 4, place, tele_ids, [near_edge, near_rest, ring_edge, ring_rest], w_qkv, "lon", q, state)
        state = attend(corner_tiles, [[0, 1], [2, 3]], 4, place, tele_ids,
                       [same_edges, other_edges], w_qkv, "corner", q, state)
        mixed = attend(across_tiles, PAIRS, 3, place, tele_ids, [far_edge, far_rest], w_qkv, "across", q, state, w_out)[0]
    else:
        q, *state = attend(own_alone, PAIRS, 2, place, tele_ids, [x], w_qkv, "own")
        same, other = lat_swap(x, n_lat)
        before = lax.ppermute(x[1:], "lon", [(i, (i + 1) % n_lon) for i in range(n_lon)])
        after = lax.ppermute(x[:1], "lon", [((i + 1) % n_lon, i) for i in range(n_lon)])
        same_edges, other_edges = lat_swap(jnp.concatenate([before, after], 0), n_lat)
        state = attend(rim_tiles, BOTH, 4, place, tele_ids, [same, other], w_qkv, "rim", q, state)
        state = attend(corner_tiles, [[0, 1], [2, 3]], 4, place, tele_ids,
                       [same_edges, other_edges], w_qkv, "corner", q, state)
        row = lax.all_gather(x, "lon", axis=0, tiled=True)
        for s in range(0, 2 * n_lon, 4):
            state = attend(functools.partial(column_tiles, s), BOTH, 4, place, tele_ids, [row[s:s + 4]], w_qkv,
                           "columns", q, state, w_out if s + 4 == 2 * n_lon else None)
        mixed = state[0]
    return mixed.reshape(tokens.shape)


def solution(mesh):
    return jax.shard_map(
        on_device,
        mesh=mesh,
        in_specs=(P("lat", "lon", None, None), P(), P(), P("lat", "lon", None)),
        out_specs=P("lat", "lon", None, None),
        check_vma=False,
    )
```
